256 devices in a mesh: head: 4 (over z_hi, core), ctx: 64 (over x, z_lo, y).
Axes of the slice: x: 4, y: 4, z: 8 (z_hi: 2, z_lo: 4; z = z_hi * 4 + z_lo), core: 2. Of those that a mesh axis runs over, the one named last changes fastest.
Arguments:
- queries: bfloat16 [32768, 8192], P(('ctx', 'head')), may hold values from -8 to 8
- keys: bfloat16 [32768, 1024], P(('ctx', 'head')), may hold values from -8 to 8
- values: bfloat16 [32768, 1024], P(('ctx', 'head')), may hold values from -6 to 6
- block_pos: int32 [256], replicated, may hold values from 0 to 255, as said below
- block_kind: int32 [256, 16], P('ctx'), may hold values from 0 to 3, as said below
- frame_span: int32 [256, 2], P('ctx'), may hold values from 0 to 256, as said below
Outputs:
- attended: bfloat16 [32768, 8192], P('ctx', 'head')
The draws below stay inside these ranges and needn't reach their ends.
Inputs may be any that keep to these rules, and one draw needn't show every extreme that they name: `block_pos`: A permutation of the sequence blocks; group c holds 2 consecutive blocks starting at r * 2 and as many starting at (127 - r) * 2, with r a permutation of the groups. `block_kind`: 0 none, 1 all, 2 causal, 3 causal or inside the frame; the entry of a block for its own slot is never 0. frame_span[b, 0] <= block_pos[b] < frame_span[b, 1].
All inputs are finite; a program needn't handle non-finite values.
Results may differ from the reference program's by a relative error of at most 0.005.
Values may be sent and summed in bfloat16 or wider, within the bound.
No kernel may reach another device: no remote copies, remote signals or barrier semaphores. Data moves between devices by JAX's collectives and lax.ppermute only.
A program may use at most 192 MiB of HBM per device.

```python
import jax
import jax.numpy as jnp
from jax import lax

QUERY_HEADS = 64
KEY_VALUE_HEADS = 8
HEAD_SIZE = 128
BLK = 128
SEG_BLK = 4
WINDOW_GROUPS = 4
GROUP_TOKENS = 512
NB = 256
SEQUENCE_LENGTH = 32768
N_CTX = 64


def folded_positions(key):
    rank_order = jax.random.permutation(jax.random.fold_in(key, 201), N_CTX).astype(jnp.int32)
    half_len = SEG_BLK // 2
    slot_index = jnp.arange(NB, dtype=jnp.int32)
    owner = slot_index // SEG_BLK
    within = slot_index % SEG_BLK
    half_index = jnp.where(within < half_len, rank_order[owner], 2 * N_CTX - 1 - rank_order[owner])
    return (half_index * half_len + within % half_len).astype(jnp.int32)


def draw_keys(key, part):
    key = jax.random.fold_in(key, 7)
    sampled_inputs = jnp.clip(jax.random.normal(key, (SEQUENCE_LENGTH, KEY_VALUE_HEADS * HEAD_SIZE), jnp.float32), -8.0, 8.0)
    return sampled_inputs.astype(jnp.bfloat16)


def draw_queries(key, part):
    key = jax.random.fold_in(key, 8)
    sampled_inputs = jnp.clip(jax.random.normal(key, (SEQUENCE_LENGTH, QUERY_HEADS * HEAD_SIZE), jnp.float32), -8.0, 8.0)
    return sampled_inputs.astype(jnp.bfloat16)


def draw_block_pos(key, part):
    return folded_positions(key)


def draw_frame_span(key, part):
    positions = folded_positions(key)
    key = jax.random.fold_in(key, 13)
    reach_back = jax.random.randint(jax.random.fold_in(key, 1), (NB,), 0, 5)
    reach_ahead = jax.random.randint(jax.random.fold_in(key, 2), (NB,), 0, 5)
    frame_lower = jnp.maximum(positions - reach_back, 0)
    frame_upper = jnp.minimum(positions + 1 + reach_ahead, NB)
    return jnp.stack([frame_lower, frame_upper], axis=1).astype(jnp.int32)


def draw_block_kind(key, part):
    key = jax.random.fold_in(key, 17)
    kind_codes = jax.random.randint(jax.random.fold_in(key, 1), (NB, WINDOW_GROUPS * SEG_BLK), 0, 4)
    own_kind = jax.random.randint(jax.random.fold_in(key, 2), (NB,), 1, 4)
    slot_index = jnp.arange(NB, dtype=jnp.int32) % SEG_BLK
    columns = jnp.arange(WINDOW_GROUPS * SEG_BLK, dtype=jnp.int32)
    kind_codes = jnp.where(columns[None, :] == slot_index[:, None], own_kind[:, None], kind_codes)
    dropped = jax.random.randint(jax.random.fold_in(key, 3), (N_CTX, WINDOW_GROUPS), 0, 2) == 0
    dropped = dropped & (jnp.arange(WINDOW_GROUPS, dtype=jnp.int32)[None, :] > 0)
    owner = jnp.arange(NB, dtype=jnp.int32) // SEG_BLK
    dropped_full = dropped[owner][:, columns // SEG_BLK]
    return jnp.where(dropped_full, 0, kind_codes).astype(jnp.int32)


def block_levels(own_key, extent, pieces, smallest, top_value):
    gain, own = 1.0, jax.random.fold_in(own_key, 6)
    for position, parts in pieces:
        steps = jnp.exp(jax.random.uniform(jax.random.fold_in(own, position), (parts,), jnp.float32, smallest / len(pieces), top_value / len(pieces)))
        gain = gain * jnp.repeat(steps, extent[position] // parts).reshape([-1 if axis == position else 1 for axis in range(len(extent))])
    return gain


def bell_draw(own_key, dims, deviation, most, pieces=(), kind=jnp.bfloat16):
    entries = deviation * jax.random.normal(own_key, dims, jnp.float32)
    if pieces:
        entries = entries * block_levels(own_key, dims, pieces, -0.22, 0.18)
    return jnp.clip(entries, -most, most).astype(kind)


def setup_inputs(seed: int = 0) -> dict:
    key_list = jax.random.split(jax.random.key(seed), 7)
    queries = draw_queries(jax.random.fold_in(key_list[6], 71), 0)
    keys = draw_keys(jax.random.fold_in(key_list[6], 71), 0)
    values = bell_draw(key_list[2], (SEQUENCE_LENGTH, KEY_VALUE_HEADS * HEAD_SIZE), 1.0, 6.0, ((0, 256),))
    block_pos = draw_block_pos(jax.random.fold_in(key_list[6], 71), 0)
    block_kind = draw_block_kind(jax.random.fold_in(key_list[6], 71), 0)
    frame_span = draw_frame_span(jax.random.fold_in(key_list[6], 71), 0)
    return {"queries": queries, "keys": keys, "values": values, "block_pos": block_pos, "block_kind": block_kind, "frame_span": frame_span}


def allowed_mask(query_pos, frame_lower, frame_upper, kind_codes, key_pos):
    kind_table = jnp.repeat(kind_codes, BLK, axis=1)
    before = key_pos[None, :] <= query_pos[:, None]
    inside = (key_pos[None, :] >= frame_lower[:, None]) & (key_pos[None, :] < frame_upper[:, None])
    return (kind_table == 1) | ((kind_table == 2) & before) | ((kind_table == 3) & (before | inside))


def reference(queries, keys, values, block_pos, block_kind, frame_span):
    group_count = QUERY_HEADS // KEY_VALUE_HEADS
    score_scale = HEAD_SIZE ** -0.5
    grouped_queries = queries.reshape(N_CTX, GROUP_TOKENS, KEY_VALUE_HEADS, group_count, HEAD_SIZE)
    grouped_keys = keys.reshape(N_CTX, GROUP_TOKENS, KEY_VALUE_HEADS, HEAD_SIZE)
    grouped_values = values.reshape(N_CTX, GROUP_TOKENS, KEY_VALUE_HEADS, HEAD_SIZE)
    block_table = block_pos.reshape(N_CTX, SEG_BLK)
    offsets = jnp.arange(GROUP_TOKENS, dtype=jnp.int32) % BLK

    def one_group(group_index):
        window_span = (group_index - jnp.arange(WINDOW_GROUPS, dtype=jnp.int32)) % N_CTX
        key_pos = jnp.repeat(block_table[window_span].reshape(-1), BLK) * BLK + jnp.tile(offsets, WINDOW_GROUPS)
        query_blocks = group_index * SEG_BLK + jnp.arange(GROUP_TOKENS, dtype=jnp.int32) // BLK
        query_pos = block_pos[query_blocks] * BLK + offsets
        frame_lower = frame_span[query_blocks, 0] * BLK
        frame_upper = frame_span[query_blocks, 1] * BLK
        allowed = allowed_mask(query_pos, frame_lower, frame_upper, block_kind[query_blocks], key_pos)
        keys_in_window = grouped_keys[window_span].reshape(WINDOW_GROUPS * GROUP_TOKENS, KEY_VALUE_HEADS, HEAD_SIZE)
        values_in_window = grouped_values[window_span].reshape(WINDOW_GROUPS * GROUP_TOKENS, KEY_VALUE_HEADS, HEAD_SIZE)
        query_block = grouped_queries[group_index]

        def single_head(head_index):
            scores = jnp.einsum("qgd,sd->gqs", query_block[:, head_index].astype(jnp.float32),
                                keys_in_window[:, head_index].astype(jnp.float32)) * score_scale
            masked = jnp.where(allowed[None], scores, -1e30)
            row_max = jnp.max(masked, axis=-1, keepdims=True)
            weights = jnp.where(allowed[None], jnp.exp(scores - row_max), 0.0)
            weight_sum = jnp.sum(weights, axis=-1)
            rounded = lax.optimization_barrier(weights.astype(jnp.bfloat16)).astype(jnp.float32)
            mixed_out = jnp.einsum("gqs,sd->gqd", rounded, values_in_window[:, head_index].astype(jnp.float32))
            return (mixed_out / weight_sum[..., None]).astype(jnp.bfloat16)

        head_outputs = lax.map(single_head, jnp.arange(KEY_VALUE_HEADS, dtype=jnp.int32))
        return jnp.transpose(head_outputs, (2, 0, 1, 3)).reshape(GROUP_TOKENS, QUERY_HEADS * HEAD_SIZE)

    return lax.map(one_group, jnp.arange(N_CTX, dtype=jnp.int32)).reshape(SEQUENCE_LENGTH, QUERY_HEADS * HEAD_SIZE)
```

```python
from functools import partial

import jax
import jax.numpy as jnp
from jax import lax
from jax.experimental import pallas as pl
from jax.experimental.pallas import tpu as pltpu
from jax.sharding import PartitionSpec as P

D = 128
BLK = 128
SEG = 4
WIN = 16
HEADS_PER_KV = 8
UNIT = HEADS_PER_KV * D
NEG = -1e30
EXP2_SCALE = (D ** -0.5) * 1.4426950408889634
VMEM_LIMIT = 48 * 1024 * 1024


def pack_kv_kernel(ids, k_ref, v_ref, own_ref, x1_ref, x2_ref, x3_ref):
    rank = ids[1]
    for m, out in enumerate((own_ref, x1_ref, x2_ref, x3_ref)):
        first = (rank ^ m) * (2 * D)
        for g in range(2):
            cols = pl.ds(pl.multiple_of(first + g * D, D), D)
            out[:, 2 * g * D : (2 * g + 1) * D] = k_ref[:, cols]
            out[:, (2 * g + 1) * D : (2 * g + 2) * D] = v_ref[:, cols]


def pack_kv(ids, keys, values):
    piece = jax.ShapeDtypeStruct((BLK, 4 * D), jnp.bfloat16)
    return pl.pallas_call(
        pack_kv_kernel,
        out_shape=[piece] * 4,
        grid_spec=pltpu.PrefetchScalarGridSpec(
            num_scalar_prefetch=1,
            grid=(1,),
            in_specs=[pl.BlockSpec((BLK, 8 * D), lambda i, ids: (0, 0))] * 2,
            out_specs=[pl.BlockSpec((BLK, 4 * D), lambda i, ids: (0, 0))] * 4,
        ),
        name="pack_kv",
    )(ids, keys, values)


def pack_q_kernel(width, dest_xor, part, ids, q_ref, dep_ref, out_ref, sem):
    first = (ids[1] ^ dest_xor) * (2 * UNIT) + part * UNIT
    copy = pltpu.make_async_copy(q_ref.at[:, pl.ds(pl.multiple_of(first, UNIT), width)], out_ref, sem)
    copy.start()
    copy.wait()


def pack_q(ids, queries, dep, dest_xor, part, width):
    return pl.pallas_call(
        partial(pack_q_kernel, width, dest_xor, part),
        out_shape=jax.ShapeDtypeStruct((BLK, width), jnp.bfloat16),
        grid_spec=pltpu.PrefetchScalarGridSpec(
            num_scalar_prefetch=1,
            grid=(1,),
            in_specs=[pl.BlockSpec(memory_space=pl.ANY)] * 2,
            out_specs=pl.BlockSpec(memory_space=pl.ANY),
            scratch_shapes=[pltpu.SemaphoreType.DMA],
        ),
        name="pack_q",
    )(ids, queries, dep)


def unit_body(chunks, count, diag, q_ref, kv, o_ref):
    keys = kv[: 2 * chunks, :, :D].reshape(2 * chunks * BLK, D)
    values = kv[: 2 * chunks, :, D:].reshape(2 * chunks * BLK, D)
    rows = lax.broadcasted_iota(jnp.int32, (2 * BLK, BLK), 0) % BLK
    cols = lax.broadcasted_iota(jnp.int32, (2 * BLK, BLK), 1)
    first_bias = jnp.where((cols > rows) & (diag > 0), NEG, 0.0)
    last_bias = jnp.where(count < 2 * chunks, NEG, 0.0)

    def pair(i, carry):
        at = [pl.ds(pl.multiple_of((2 * i + e) * D, D), D) for e in range(2)]
        q2 = jnp.concatenate([q_ref[:, at[0]], q_ref[:, at[1]]], axis=0)
        scores = lax.dot_general(q2, keys, (((1,), (1,)), ((), ())), preferred_element_type=jnp.float32)
        blocks = [scores[:, j * BLK : (j + 1) * BLK] for j in range(2 * chunks)]
        blocks[0] = blocks[0] + first_bias
        blocks[-1] = blocks[-1] + last_bias
        top = blocks[0]
        for b in blocks[1:]:
            top = jnp.maximum(top, b)
        top = jnp.max(top, axis=1, keepdims=True)
        weights = [jnp.exp2((b - top) * EXP2_SCALE) for b in blocks]
        total = weights[0]
        for w in weights[1:]:
            total = total + w
        total = jnp.sum(total, axis=1, keepdims=True)
        rounded = jnp.concatenate([w.astype(jnp.bfloat16) for w in weights], axis=1)
        mixed = lax.dot_general(rounded, values, (((1,), (0,)), ((), ())), preferred_element_type=jnp.float32)
        result = (mixed / total).astype(jnp.bfloat16)
        o_ref[:, at[0]] = result[:BLK]
        o_ref[:, at[1]] = result[BLK:]
        return carry

    lax.fori_loop(0, HEADS_PER_KV // 2, pair, 0)


def attend_kernel(block_xor, part, ids, block_pos, block_kind, frame_span, q_ref, s0, s1, s2, s3, prev, o_ref, kv, sem):
    ctx, rank = ids[0], ids[1]
    head = pl.program_id(0) + part
    row_block = rank ^ block_xor
    own_pos = block_pos[ctx * SEG + row_block]
    lower = frame_span[2 * row_block]
    upper = frame_span[2 * row_block + 1]
    cols = pl.ds(pl.multiple_of(head * (2 * D), 2 * D), 2 * D)

    def fetch(slot, m, to):
        return pltpu.make_async_copy(slot.at[m, :, cols], kv.at[to], sem)

    fetch(s0, block_xor, 0).start()
    own_kind = block_kind[row_block * WIN + row_block]
    count = jnp.int32(1)
    for s, slot in enumerate((s0, s1, s2, s3)):
        group = lax.rem(ctx - s + 64, 64)
        for m in range(SEG):
            if s == 0 and m == block_xor:
                continue
            u = rank ^ m
            kind = block_kind[row_block * WIN + s * SEG + u]
            pos = block_pos[group * SEG + u]
            before = pos < own_pos
            inside = (pos >= lower) & (pos < upper)
            live = (kind == 1) | ((kind == 2) & before) | ((kind == 3) & (before | inside))

            @pl.when(live)
            def _(slot=slot, m=m, count=count):
                fetch(slot, m, count).start()

            count = count + live.astype(jnp.int32)
    odd = lax.rem(count, 2) == 1

    @pl.when(odd)
    def _():
        fetch(s0, block_xor, count).start()

    chunks = (count + 1) // 2

    def wait(i, carry):
        fetch(s0, block_xor, 0).wait()
        return carry

    lax.fori_loop(0, 2 * chunks, wait, 0)
    diag = (own_kind == 2).astype(jnp.int32)
    for c in range(1, WIN // 2 + 1):
        @pl.when(chunks == c)
        def _(c=c):
            unit_body(c, count, diag, q_ref, kv, o_ref)


def attend(scalars, q, q_index, slots, prev, block_xor, part, parts):
    out_shape = jax.ShapeDtypeStruct((SEG * BLK, 2 * UNIT), jnp.bfloat16)
    aliases = {}
    operands = [*scalars, q, *slots]
    in_specs = [pl.BlockSpec((BLK, UNIT), q_index)] + [pl.BlockSpec(memory_space=pl.ANY)] * 4
    body = partial(attend_kernel, block_xor, part)
    if prev is None:
        inner = body

        def body(*refs):
            return inner(*refs[:9], None, *refs[9:])
    else:
        operands.append(prev)
        in_specs.append(pl.BlockSpec(memory_space=pl.ANY))
        aliases = {len(operands) - 1: 0}
    return pl.pallas_call(
        body,
        out_shape=out_shape,
        grid_spec=pltpu.PrefetchScalarGridSpec(
            num_scalar_prefetch=4,
            grid=(parts,),
            in_specs=in_specs,
            out_specs=pl.BlockSpec((BLK, UNIT), lambda i, ids, *_: (ids[1] ^ block_xor, part + i)),
            scratch_shapes=[pltpu.VMEM((WIN, BLK, 2 * D), jnp.bfloat16), pltpu.SemaphoreType.DMA],
        ),
        input_output_aliases=aliases,
        compiler_params=pltpu.CompilerParams(vmem_limit_bytes=VMEM_LIMIT),
        cost_estimate=pl.CostEstimate(flops=parts * 600_000_000, bytes_accessed=parts * 1_500_000, transcendentals=parts * 1_000_000),
        name="attend",
    )(*operands)


def body(queries, keys, values, block_pos, block_kind, frame_span):
    ctx, rank = lax.axis_index("ctx"), lax.axis_index("head")
    groups = lax.axis_size("ctx")
    ranks = lax.axis_size("head")
    y = ctx % 4
    ids = jnp.stack([ctx, rank]).astype(jnp.int32)
    scalars = (ids, block_pos, block_kind.reshape(-1), frame_span.reshape(-1))

    def swap(value, m):
        return lax.ppermute(value, "head", [(i, i ^ m) for i in range(ranks)])

    def ring(value, by):
        return lax.ppermute(value, "ctx", [(i, i // 4 * 4 + (i + by) % 4) for i in range(groups)])

    own, x1, x2, x3 = pack_kv(ids, keys, values)
    from2, from3, from1 = swap(x2, 2), swap(x3, 3), swap(x1, 1)
    kv0 = jnp.stack([own, from1, from2, from3])
    late = lax.ppermute(kv0, "ctx", [(i, (i + 4) % groups) for i in range(groups) if i % 4])
    kv1 = ring(jnp.where(y == 3, late, kv0), 1)
    kv3 = ring(jnp.where(y == 0, kv0, late), 3)
    kv2 = ring(jnp.where(y >= 2, late, kv0), 2)
    slots = (kv0, kv1, kv2, kv3)

    q1 = swap(pack_q(ids, queries, ids, 1, 0, 2 * UNIT), 1)
    a = swap(pack_q(ids, queries, from2, 2, 0, UNIT), 2)
    b = swap(pack_q(ids, queries, late, 3, 0, UNIT), 3)
    c = swap(pack_q(ids, queries, a, 2, 1, UNIT), 2)
    d = swap(pack_q(ids, queries, b, 3, 1, UNIT), 3)

    out = attend(scalars, queries, lambda i, ids, *_: (0, 2 * ids[1] + i), slots, None, 0, 0, 2)
    out = attend(scalars, q1, lambda i, *_: (0, i), slots, out, 1, 0, 2)
    for m, part, q in ((2, 0, a), (3, 0, b), (2, 1, c), (3, 1, d)):
        out = attend(scalars, q, lambda i, *_: (0, 0), slots, out, m, part, 1)
    return out


def solution(mesh):
    in_specs = (
        P(("ctx", "head"), None),
        P(("ctx", "head"), None),
        P(("ctx", "head"), None),
        P(),
        P("ctx", None),
        P("ctx", None),
    )
    out_specs = P("ctx", "head")
    return jax.shard_map(body, mesh=mesh, in_specs=in_specs, out_specs=out_specs, check_vma=False)
```

```python
from functools import partial

import jax
import jax.numpy as jnp
from jax import lax
from jax.experimental import pallas as pl
from jax.experimental.pallas import tpu as pltpu
from jax.sharding import PartitionSpec as P

D = 128
BLK = 128
SEG = 4
WIN = 16
HEADS_PER_KV = 8
UNIT = HEADS_PER_KV * D
GROUPS = 64
NEG = -1e30
EXP2_SCALE = (D ** -0.5) * 1.4426950408889634
VMEM_LIMIT = 40 * 1024 * 1024
PLAN = WIN + 2
VMEM = pl.BlockSpec(memory_space=pltpu.VMEM)
SMEM = pl.BlockSpec(memory_space=pltpu.SMEM)
ANY = pl.BlockSpec(memory_space=pl.ANY)


def bf16(*shape):
    return jax.ShapeDtypeStruct(shape, jnp.bfloat16)


def plan_kernel(ids, block_pos, block_kind, frame_span, plan):
    ctx, rank = ids[0], ids[1]
    for block_xor in range(SEG):
        row_block = rank ^ block_xor
        own_pos = block_pos[ctx * SEG + row_block]
        lower = frame_span[row_block, 0]
        upper = frame_span[row_block, 1]
        base = block_xor * PLAN
        plan[base + 1] = (block_kind[row_block, row_block] == 2).astype(jnp.int32)
        plan[base + 2 + block_xor] = jnp.int32(0)
        count = jnp.int32(1)
        for s in range(SEG):
            group = lax.rem(ctx - s + GROUPS, GROUPS)
            for m in range(SEG):
                if s == 0 and m == block_xor:
                    continue
                u = rank ^ m
                kind = block_kind[row_block, s * SEG + u]
                pos = block_pos[group * SEG + u]
                before = pos < own_pos
                inside = (pos >= lower) & (pos < upper)
                live = (kind == 1) | ((kind == 2) & before) | ((kind == 3) & (before | inside))
                plan[base + 2 + s * SEG + m] = jnp.where(live, count, -1)
                count = count + live.astype(jnp.int32)
        plan[base] = count


def make_plan(ids, block_pos, block_kind, frame_span):
    return pl.pallas_call(
        plan_kernel,
        out_shape=jax.ShapeDtypeStruct((SEG * PLAN,), jnp.int32),
        in_specs=[SMEM] * 4,
        out_specs=SMEM,
        name="plan",
    )(ids, block_pos, block_kind, frame_span)


def pack_kv_kernel(ids, k_ref, v_ref, own_ref, x1_ref, x2_ref, x3_ref):
    for m, out in enumerate((own_ref, x1_ref, x2_ref, x3_ref)):
        first = (ids[1] ^ m) * (2 * D)
        for g in range(2):
            cols = pl.ds(pl.multiple_of(first + g * D, D), D)
            out[:, 2 * g * D : (2 * g + 1) * D] = k_ref[:, cols]
            out[:, (2 * g + 1) * D : (2 * g + 2) * D] = v_ref[:, cols]


def pack_kv(ids, keys, values):
    return pl.pallas_call(
        pack_kv_kernel,
        out_shape=[bf16(BLK, 4 * D)] * 4,
        in_specs=[SMEM, VMEM, VMEM],
        out_specs=[VMEM] * 4,
        name="pack_kv",
    )(ids, keys, values)


def pack_q_kernel(ids, q_ref, own_ref, x1_ref, a_ref, b_ref, c_ref, d_ref):
    for out, m, part in ((a_ref, 2, 0), (b_ref, 3, 0), (x1_ref, 1, 0), (own_ref, 0, 0), (c_ref, 2, 1), (d_ref, 3, 1)):
        first = (ids[1] ^ m) * (2 * UNIT) + part * UNIT
        out[...] = q_ref[:, pl.ds(pl.multiple_of(first, UNIT), out.shape[1])]


def pack_q(ids, queries):
    return pl.pallas_call(
        pack_q_kernel,
        out_shape=[bf16(BLK, 2 * UNIT)] * 2 + [bf16(BLK, UNIT)] * 4,
        in_specs=[SMEM, VMEM],
        out_specs=[VMEM] * 6,
        name="pack_q",
    )(ids, queries)


def gate(value, dep):
    return pl.pallas_call(
        lambda value_ref, dep_ref, out_ref: None,
        out_shape=jax.ShapeDtypeStruct(value.shape, value.dtype),
        in_specs=[ANY, ANY],
        out_specs=ANY,
        input_output_aliases={0: 0},
        name="gate",
    )(value, dep)


def unit_body(chunks, count, diag, q_ref, kv, o_ref):
    keys = kv[: 2 * chunks, :, :D].reshape(2 * chunks * BLK, D)
    values = kv[: 2 * chunks, :, D:].reshape(2 * chunks * BLK, D)
    rows = lax.broadcasted_iota(jnp.int32, (2 * BLK, BLK), 0) % BLK
    cols = lax.broadcasted_iota(jnp.int32, (2 * BLK, BLK), 1)
    first_bias = jnp.where((cols > rows) & (diag > 0), NEG, 0.0)
    last_bias = jnp.where(count < 2 * chunks, NEG, 0.0)

    def pair(i, carry):
        at = [pl.ds(pl.multiple_of((2 * i + e) * D, D), D) for e in range(2)]
        q2 = jnp.concatenate([q_ref[:, at[0]], q_ref[:, at[1]]], axis=0)
        scores = lax.dot_general(q2, keys, (((1,), (1,)), ((), ())), preferred_element_type=jnp.float32)
        blocks = [scores[:, j * BLK : (j + 1) * BLK] for j in range(2 * chunks)]
        blocks[0] = blocks[0] + first_bias
        blocks[-1] = blocks[-1] + last_bias
        top = blocks[0]
        for b in blocks[1:]:
            top = jnp.maximum(top, b)
        top = jnp.max(top, axis=1, keepdims=True)
        weights = [jnp.exp2((b - top) * EXP2_SCALE) for b in blocks]
        total = weights[0]
        for w in weights[1:]:
            total = total + w
        total = jnp.sum(total, axis=1, keepdims=True)
        rounded = jnp.concatenate([w.astype(jnp.bfloat16) for w in weights], axis=1)
        mixed = lax.dot_general(rounded, values, (((1,), (0,)), ((), ())), preferred_element_type=jnp.float32)
        result = (mixed / total).astype(jnp.bfloat16)
        o_ref[:, at[0]] = result[:BLK]
        o_ref[:, at[1]] = result[BLK:]
        return carry

    lax.fori_loop(0, HEADS_PER_KV // 2, pair, 0)


def attend_kernel(units, n_q, has_prev, ids, plan, *refs):
    qs, halves = refs[:n_q], refs[n_q : n_q + 2 * SEG]
    out, q_now, kv, o_buf, sems = refs[n_q + 2 * SEG + has_prev :]
    rank = ids[1]

    def target(i):
        _, _, m, g = units[i]
        rows = pl.ds(pl.multiple_of((rank ^ m) * BLK, BLK), BLK)
        return pltpu.make_async_copy(o_buf.at[i], out.at[rows, g * UNIT : (g + 1) * UNIT], sems.at[i])

    def unit(i, carry):
        count, diag = jnp.int32(0), jnp.int32(0)
        for n, (q, part, m, g) in enumerate(units):
            base = m * PLAN
            count = jnp.where(i == n, plan[base], count)
            diag = jnp.where(i == n, plan[base + 1], diag)

            @pl.when(i == n)
            def _(q=q, part=part, m=m, g=g, base=base):
                q_now[...] = qs[q][:, part * UNIT : (part + 1) * UNIT]
                cols = slice(2 * g * D, 2 * (g + 1) * D)
                for code in range(WIN):
                    place = plan[base + 2 + code]

                    @pl.when(place >= 0)
                    def _(code=code, place=place):
                        kv[place] = halves[code // 2][code % 2, :, cols]

                @pl.when(lax.rem(plan[base], 2) == 1)
                def _():
                    kv[plan[base]] = halves[m // 2][m % 2, :, cols]

        chunks = (count + 1) // 2
        for c in range(1, WIN // 2 + 1):
            @pl.when(chunks == c)
            def _(c=c):
                unit_body(c, count, diag, q_now, kv, o_buf.at[i])
        for n in range(len(units)):
            @pl.when(i == n)
            def _(n=n):
                target(n).start()
        return carry

    lax.fori_loop(0, len(units), unit, 0)
    for n in range(len(units)):
        target(n).wait()


def attend(ids, plan, qs, units, halves, prev):
    operands = [ids, plan, *qs, *halves]
    in_specs = [SMEM] * 2 + [VMEM] * (len(qs) + len(halves))
    aliases = {}
    if prev is not None:
        aliases = {len(operands): 0}
        operands.append(prev)
        in_specs.append(ANY)
    n = len(units)
    return pl.pallas_call(
        partial(attend_kernel, units, len(qs), int(prev is not None)),
        out_shape=bf16(SEG * BLK, 2 * UNIT),
        in_specs=in_specs,
        out_specs=ANY,
        scratch_shapes=[
            pltpu.VMEM((BLK, UNIT), jnp.bfloat16),
            pltpu.VMEM((WIN, BLK, 2 * D), jnp.bfloat16),
            pltpu.VMEM((n, BLK, UNIT), jnp.bfloat16),
            pltpu.SemaphoreType.DMA((n,)),
        ],
        input_output_aliases=aliases,
        compiler_params=pltpu.CompilerParams(vmem_limit_bytes=VMEM_LIMIT),
        cost_estimate=pl.CostEstimate(flops=n * 600_000_000, bytes_accessed=n * 1_500_000, transcendentals=n * 1_000_000),
        name="attend",
    )(*operands)


def body(queries, keys, values, block_pos, block_kind, frame_span):
    ctx, rank = lax.axis_index("ctx"), lax.axis_index("head")
    groups = lax.axis_size("ctx")
    ranks = lax.axis_size("head")
    y = ctx % 4
    ids = jnp.stack([ctx, rank]).astype(jnp.int32)

    def swap(value, m):
        return lax.ppermute(value, "head", [(i, i ^ m) for i in range(ranks)])

    def ring(value, by):
        return lax.ppermute(value, "ctx", [(i, i // 4 * 4 + (i + by) % 4) for i in range(groups)])

    def window(half):
        late = lax.ppermute(half, "ctx", [(i, (i + 4) % groups) for i in range(groups) if i % 4])
        one = ring(jnp.where(y == 3, late, half), 1)
        three = ring(jnp.where(y == 0, half, late), 3)
        two = ring(jnp.where(y >= 2, late, half), 2)
        return (half, one, two, three), late

    own, x1, x2, x3 = pack_kv(ids, keys, values)
    from1 = swap(x1, 1)
    from2, from3 = swap(x2, 2), swap(x3, 3)
    near, near_late = window(jnp.stack([own, from1]))
    far, far_late = window(jnp.stack([from2, from3]))
    halves = [h for pair in zip(near, far) for h in pair]

    q0, q1, a, b, c, d = pack_q(ids, queries)
    q1 = swap(q1, 1)
    a = swap(gate(a, near_late), 2)
    b = swap(gate(b, from2), 3)
    c = swap(gate(c, far_late), 2)
    d = swap(gate(d, a), 3)

    plan = make_plan(ids, block_pos, block_kind, frame_span)
    out = attend(ids, plan, (q0, q1), ((0, 0, 0, 0), (0, 1, 0, 1), (1, 0, 1, 0), (1, 1, 1, 1)), halves, None)
    out = attend(ids, plan, (a, b), ((0, 0, 2, 0), (1, 0, 3, 0)), halves, out)
    out = attend(ids, plan, (c,), ((0, 0, 2, 1),), halves, out)
    out = attend(ids, plan, (d,), ((0, 0, 3, 1),), halves, out)
    return out


def solution(mesh):
    in_specs = (
        P(("ctx", "head"), None),
        P(("ctx", "head"), None),
        P(("ctx", "head"), None),
        P(),
        P("ctx", None),
        P("ctx", None),
    )
    out_specs = P("ctx", "head")
    return jax.shard_map(body, mesh=mesh, in_specs=in_specs, out_specs=out_specs, check_vma=False)
```

```python
from functools import partial

import jax
import jax.numpy as jnp
from jax import lax
from jax.experimental import pallas as pl
from jax.experimental.pallas import tpu as pltpu
from jax.sharding import PartitionSpec as P

D = 128
BLK = 128
SEG = 4
WIN = 16
HEADS_PER_KV = 8
UNIT = HEADS_PER_KV * D
GROUPS = 64
NEG = -1e30
EXP2_SCALE = (D ** -0.5) * 1.4426950408889634
VMEM_LIMIT = 16 * 1024 * 1024
PLAN = WIN + 2
VMEM = pl.BlockSpec(memory_space=pltpu.VMEM)
SMEM = pl.BlockSpec(memory_space=pltpu.SMEM)
ANY = pl.BlockSpec(memory_space=pl.ANY)
TINY = pl.CostEstimate(flops=1000, bytes_accessed=1000, transcendentals=0)


def bf16(*shape):
    return jax.ShapeDtypeStruct(shape, jnp.bfloat16)


def place():
    return lax.axis_index("ctx"), lax.axis_index("head")


def plan_kernel(block_pos, block_kind, frame_span, plan):
    ctx, rank = place()
    for block_xor in range(SEG):
        row_block = rank ^ block_xor
        own_pos = block_pos[ctx * SEG + row_block]
        lower = frame_span[row_block, 0]
        upper = frame_span[row_block, 1]
        base = block_xor * PLAN
        plan[base + 1] = (block_kind[row_block, row_block] == 2).astype(jnp.int32)
        plan[base + 2 + block_xor] = jnp.int32(0)
        count = jnp.int32(1)
        for s in range(SEG):
            group = lax.rem(ctx - s + GROUPS, GROUPS)
            for m in range(SEG):
                if s == 0 and m == block_xor:
                    continue
                u = rank ^ m
                kind = block_kind[row_block, s * SEG + u]
                pos = block_pos[group * SEG + u]
                before = pos < own_pos
                inside = (pos >= lower) & (pos < upper)
                live = (kind == 1) | ((kind == 2) & before) | ((kind == 3) & (before | inside))
                plan[base + 2 + s * SEG + m] = jnp.where(live, count, -1)
                count = count + live.astype(jnp.int32)
        plan[base] = count


def make_plan(block_pos, block_kind, frame_span):
    return pl.pallas_call(
        plan_kernel,
        out_shape=jax.ShapeDtypeStruct((SEG * PLAN,), jnp.int32),
        in_specs=[SMEM] * 3,
        out_specs=SMEM,
        cost_estimate=TINY,
        name="plan",
    )(block_pos, block_kind, frame_span)


def pack_kv_kernel(k_ref, v_ref, own_ref, x1_ref, x2_ref, x3_ref):
    _, rank = place()
    for m, out in enumerate((own_ref, x1_ref, x2_ref, x3_ref)):
        for g in range(2):
            cols = pl.ds(pl.multiple_of((rank ^ m) * (2 * D) + g * D, D), D)
            out[:, 2 * g * D : (2 * g + 1) * D] = k_ref[:, cols]
            out[:, (2 * g + 1) * D : (2 * g + 2) * D] = v_ref[:, cols]


def pack_kv(keys, values):
    return pl.pallas_call(
        pack_kv_kernel,
        out_shape=[bf16(BLK, 4 * D)] * 4,
        in_specs=[VMEM, VMEM],
        out_specs=[VMEM] * 4,
        cost_estimate=TINY,
        name="pack_kv",
    )(keys, values)


def pack_q_kernel(q_ref, dep_ref, own_ref, x1_ref, a_ref, b_ref, c_ref, d_ref):
    _, rank = place()
    for out, m, part in ((a_ref, 2, 0), (b_ref, 3, 0), (x1_ref, 1, 0), (own_ref, 0, 0), (c_ref, 2, 1), (d_ref, 3, 1)):
        first = (rank ^ m) * (2 * UNIT) + part * UNIT
        out[...] = q_ref[:, pl.ds(pl.multiple_of(first, UNIT), out.shape[1])]


def pack_q(queries, dep):
    return pl.pallas_call(
        pack_q_kernel,
        out_shape=[bf16(BLK, 2 * UNIT)] * 2 + [bf16(BLK, UNIT)] * 4,
        in_specs=[VMEM, SMEM],
        out_specs=[VMEM] * 6,
        cost_estimate=TINY,
        name="pack_q",
    )(queries, dep)


def gate(value, *deps):
    return pl.pallas_call(
        lambda *refs: None,
        out_shape=jax.ShapeDtypeStruct(value.shape, value.dtype),
        in_specs=[ANY] * (1 + len(deps)),
        out_specs=ANY,
        input_output_aliases={0: 0},
        cost_estimate=TINY,
        name="gate",
    )(value, *deps)


ROWS = HEADS_PER_KV * BLK
TILE = 256
CH = 4
SAFE = 2.0 ** 80


def block_bias(bias, at, count):
    return bias[jnp.where(at >= count, 2, jnp.where(at == 0, 0, 1))]


def weigh_step(width, first, count, q_ref, kv, total, acc, bias):
    keys = kv[pl.ds(first, width), :, :D].reshape(width * BLK, D)
    values = kv[pl.ds(first, width), :, D:].reshape(width * BLK, D)
    more = first > 0

    def score(t):
        return lax.dot_general(q_ref[t : t + TILE], keys, (((1,), (1,)), ((), ())), preferred_element_type=jnp.float32)

    def weigh(t, scores):
        rounded = []
        for r in range(0, TILE, BLK):
            weights = [
                jnp.exp2(scores[r : r + BLK, e * BLK : (e + 1) * BLK] * EXP2_SCALE + block_bias(bias, first + e, count))
                for e in range(width)
            ]
            part = weights[0]
            for w in weights[1:]:
                part = part + w
            rows = slice(t + r, t + r + BLK)
            total[rows] = jnp.where(more, total[rows], 0.0) + part
            rounded.append(jnp.concatenate([w.astype(jnp.bfloat16) for w in weights], axis=1))
        return jnp.concatenate(rounded, axis=0)

    tiles = list(range(0, ROWS, TILE))
    ahead = score(tiles[0])
    for n, t in enumerate(tiles):
        now = ahead
        if n + 1 < len(tiles):
            ahead = score(tiles[n + 1])
        mixed = lax.dot_general(weigh(t, now), values, (((1,), (0,)), ((), ())), preferred_element_type=jnp.float32)
        acc[t : t + TILE] = jnp.where(more, acc[t : t + TILE], 0.0) + mixed


def fast_unit(count, q_ref, kv, total, acc, bias, low, high, o_ref):
    wide = count // CH
    rest = count - wide * CH
    wide = wide + (rest > 2).astype(jnp.int32)

    def step(j, carry):
        weigh_step(CH, CH * j, count, q_ref, kv, total, acc, bias)
        return carry

    lax.fori_loop(0, wide, step, 0)

    @pl.when((rest == 1) | (rest == 2))
    def _():
        weigh_step(2, CH * wide, count, q_ref, kv, total, acc, bias)

    least, most = low[...], high[...]
    for h in range(HEADS_PER_KV):
        r = slice(h * BLK, (h + 1) * BLK)
        weight_sum = jnp.sum(total[r], axis=1, keepdims=True)
        least = jnp.minimum(least, weight_sum)
        most = jnp.maximum(most, weight_sum)
        o_ref[:, h * D : (h + 1) * D] = (acc[r] / weight_sum).astype(jnp.bfloat16)
    low[...] = least
    high[...] = most


def safe_unit(count, q_ref, kv, bias, o_ref):
    chunks = (count + CH - 1) // CH

    def head(h, carry):
        q = q_ref[pl.ds(pl.multiple_of(h * BLK, BLK), BLK)]

        def scaled(j):
            keys = kv[pl.ds(CH * j, CH), :, :D].reshape(CH * BLK, D)
            scores = lax.dot_general(q, keys, (((1,), (1,)), ((), ())), preferred_element_type=jnp.float32)
            return [
                scores[:, e * BLK : (e + 1) * BLK] * EXP2_SCALE + block_bias(bias, CH * j + e, count) for e in range(CH)
            ]

        def largest(j, top):
            for block in scaled(j):
                top = jnp.maximum(top, block)
            return top

        top = lax.fori_loop(0, chunks, largest, jnp.full((BLK, BLK), 2 * NEG, jnp.float32))
        top = jnp.max(top, axis=1, keepdims=True)

        def step(j, carry):
            part, mix = carry
            values = kv[pl.ds(CH * j, CH), :, D:].reshape(CH * BLK, D)
            weights = [jnp.exp2(block - top) for block in scaled(j)]
            for w in weights:
                part = part + w
            rounded = jnp.concatenate([w.astype(jnp.bfloat16) for w in weights], axis=1)
            mix = mix + lax.dot_general(rounded, values, (((1,), (0,)), ((), ())), preferred_element_type=jnp.float32)
            return part, mix

        zero = jnp.zeros((BLK, BLK), jnp.float32)
        part, mix = lax.fori_loop(0, chunks, step, (zero, zero))
        o_ref[:, pl.ds(pl.multiple_of(h * D, D), D)] = (mix / jnp.sum(part, axis=1, keepdims=True)).astype(jnp.bfloat16)
        return carry

    lax.fori_loop(0, HEADS_PER_KV, head, 0)


def attend_kernel(g, units, n_q, has_prev, plan, *refs):
    qs, slots = refs[:n_q], refs[n_q : n_q + SEG]
    out, q_now, kv, total, acc, bias, low, high, o_buf, sems = refs[n_q + SEG + has_prev :]
    _, rank = place()

    def target(i):
        rows = pl.ds(pl.multiple_of((rank ^ units[i][2]) * BLK, BLK), BLK)
        return pltpu.make_async_copy(o_buf.at[i], out.at[rows, g * UNIT : (g + 1) * UNIT], sems.at[i])

    rows = lax.broadcasted_iota(jnp.int32, (BLK, BLK), 0)
    cols = lax.broadcasted_iota(jnp.int32, (BLK, BLK), 1)
    bias[1] = jnp.zeros((BLK, BLK), jnp.float32)
    bias[2] = jnp.full((BLK, BLK), NEG, jnp.float32)
    low[...] = jnp.full((BLK, 1), SAFE, jnp.float32)
    high[...] = jnp.zeros((BLK, 1), jnp.float32)

    def gather(i):
        count, diag = jnp.int32(0), jnp.int32(0)
        for n, (q, part, m) in enumerate(units):
            base = m * PLAN
            count = jnp.where(i == n, plan[base], count)
            diag = jnp.where(i == n, plan[base + 1], diag)

            @pl.when(i == n)
            def _(q=q, part=part, m=m, base=base):
                for h in range(HEADS_PER_KV):
                    q_now[h * BLK : (h + 1) * BLK] = qs[q][:, part * UNIT + h * D : part * UNIT + (h + 1) * D]
                for code in range(WIN):
                    to = plan[base + 2 + code]

                    @pl.when(to >= 0)
                    def _(code=code, to=to):
                        kv[to] = slots[code // SEG][code % SEG]

                rest = lax.rem(plan[base], CH)
                for more in range(CH - 1):
                    @pl.when((rest != 0) & (rest + more < CH))
                    def _(more=more):
                        kv[plan[base] + more] = slots[0][m]

        bias[0] = jnp.where((cols > rows) & (diag > 0), NEG, 0.0)
        return count

    def fast(i, carry):
        count = gather(i)
        fast_unit(count, q_now, kv, total, acc, bias, low, high, o_buf.at[i])
        return carry

    def safe(i, carry):
        count = gather(i)
        safe_unit(count, q_now, kv, bias, o_buf.at[i])
        return carry

    lax.fori_loop(0, len(units), fast, 0)
    inside = (jnp.min(low[...]) > 1 / SAFE) & (jnp.max(high[...]) < SAFE)

    @pl.when(jnp.logical_not(inside))
    def _():
        lax.fori_loop(0, len(units), safe, 0)

    for n in range(len(units)):
        target(n).start()
    for n in range(len(units)):
        target(n).wait()


def attend(plan, g, qs, units, slots, prev):
    operands = [plan, *qs, *slots]
    in_specs = [SMEM] + [VMEM] * (len(qs) + len(slots))
    aliases = {}
    if prev is not None:
        aliases = {len(operands): 0}
        operands.append(prev)
        in_specs.append(ANY)
    n = len(units)
    return pl.pallas_call(
        partial(attend_kernel, g, units, len(qs), int(prev is not None)),
        out_shape=bf16(SEG * BLK, 2 * UNIT),
        in_specs=in_specs,
        out_specs=ANY,
        scratch_shapes=[
            pltpu.VMEM((ROWS, D), jnp.bfloat16),
            pltpu.VMEM((WIN, BLK, 2 * D), jnp.bfloat16),
            pltpu.VMEM((ROWS, BLK), jnp.float32),
            pltpu.VMEM((ROWS, D), jnp.float32),
            pltpu.VMEM((3, BLK, BLK), jnp.float32),
            pltpu.VMEM((BLK, 1), jnp.float32),
            pltpu.VMEM((BLK, 1), jnp.float32),
            pltpu.VMEM((n, BLK, UNIT), jnp.bfloat16),
            pltpu.SemaphoreType.DMA((n,)),
        ],
        input_output_aliases=aliases,
        compiler_params=pltpu.CompilerParams(vmem_limit_bytes=VMEM_LIMIT),
        cost_estimate=TINY,
        name="attend",
    )(*operands)


def body(queries, keys, values, block_pos, block_kind, frame_span):
    groups = lax.axis_size("ctx")
    ranks = lax.axis_size("head")
    y = lax.axis_index("ctx") % 4

    def swap(value, m):
        return lax.ppermute(value, "head", [(i, i ^ m) for i in range(ranks)])

    def ring(value, by):
        return lax.ppermute(value, "ctx", [(i, i // 4 * 4 + (i + by) % 4) for i in range(groups)])

    def plane(value):
        return lax.ppermute(value, "ctx", [(i, (i + 4) % groups) for i in range(groups) if i % 4])

    own, x1, x2, x3 = pack_kv(keys, values)
    plan = make_plan(block_pos, block_kind, frame_span)
    q0, q1, a, b, c, d = pack_q(queries, plan)
    from1, from2, from3 = swap(x1, 1), swap(x2, 2), swap(x3, 3)
    pieces = (own, from1, from2, gate(from3, q0))

    def group(g):
        return jnp.stack([piece[:, 2 * g * D : 2 * (g + 1) * D] for piece in pieces])

    def choose(kv, late):
        return jnp.where(y == 3, late, kv), jnp.where(y >= 2, late, kv), jnp.where(y == 0, kv, late)

    def rings(sent):
        return [ring(value, by) for by, value in zip((1, 2, 3), sent)]

    kv0, kv1 = group(0), group(1)
    late0, late1 = plane(kv0), plane(kv1)
    a = swap(gate(a, late0), 2)
    b = swap(gate(b, late1), 3)
    slots0 = [kv0, *rings(choose(kv0, late0))]
    q1 = swap(q1, 1)
    mark = swap(gate(own[:16, :D], a), 1)
    sent1 = choose(kv1, gate(late1, mark, *slots0[1:]))
    slots1 = [kv1, *rings(sent1)]
    q0 = gate(q0, *sent1)
    c = swap(gate(c, a), 2)

    out = attend(plan, 0, (q0, q1), ((0, 0, 0), (1, 0, 1)), slots0, None)
    d = swap(gate(d, b, out), 3)
    out = attend(plan, 1, (q0, q1), ((0, 1, 0), (1, 1, 1)), slots1, out)
    out = attend(plan, 0, (a, b), ((0, 0, 2), (1, 0, 3)), slots0, out)
    out = attend(plan, 1, (c, d), ((0, 0, 2), (1, 0, 3)), slots1, out)
    return out


def solution(mesh):
    in_specs = (
        P(("ctx", "head"), None),
        P(("ctx", "head"), None),
        P(("ctx", "head"), None),
        P(),
        P("ctx", None),
        P("ctx", None),
    )
    out_specs = P("ctx", "head")
    return jax.shard_map(body, mesh=mesh, in_specs=in_specs, out_specs=out_specs, check_vma=False)
```

```python
from functools import partial

import jax
import jax.numpy as jnp
from jax import lax
from jax.experimental import pallas as pl
from jax.experimental.pallas import tpu as pltpu
from jax.sharding import PartitionSpec as P

D = 128
BLK = 128
SEG = 4
WIN = 16
HEADS_PER_KV = 8
UNIT = HEADS_PER_KV * D
GROUPS = 64
NEG = -1e30
EXP2_SCALE = (D ** -0.5) * 1.4426950408889634
VMEM_LIMIT = 16 * 1024 * 1024
PLAN = WIN + 2
VMEM = pl.BlockSpec(memory_space=pltpu.VMEM)
SMEM = pl.BlockSpec(memory_space=pltpu.SMEM)
ANY = pl.BlockSpec(memory_space=pl.ANY)
TINY = pl.CostEstimate(flops=1000, bytes_accessed=1000, transcendentals=0)


def bf16(*shape):
    return jax.ShapeDtypeStruct(shape, jnp.bfloat16)


def place():
    return lax.axis_index("ctx"), lax.axis_index("head")


def plan_kernel(block_pos, block_kind, frame_span, plan):
    ctx, rank = place()
    for block_xor in range(SEG):
        row_block = rank ^ block_xor
        own_pos = block_pos[ctx * SEG + row_block]
        lower = frame_span[row_block, 0]
        upper = frame_span[row_block, 1]
        base = block_xor * PLAN
        plan[base + 1] = (block_kind[row_block, row_block] == 2).astype(jnp.int32)
        plan[base + 2 + block_xor] = jnp.int32(0)
        count = jnp.int32(1)
        for s in range(SEG):
            group = lax.rem(ctx - s + GROUPS, GROUPS)
            for m in range(SEG):
                if s == 0 and m == block_xor:
                    continue
                u = rank ^ m
                kind = block_kind[row_block, s * SEG + u]
                pos = block_pos[group * SEG + u]
                before = pos < own_pos
                inside = (pos >= lower) & (pos < upper)
                live = (kind == 1) | ((kind == 2) & before) | ((kind == 3) & (before | inside))
                plan[base + 2 + s * SEG + m] = jnp.where(live, count, -1)
                count = count + live.astype(jnp.int32)
        plan[base] = count


def make_plan(block_pos, block_kind, frame_span):
    return pl.pallas_call(
        plan_kernel,
        out_shape=jax.ShapeDtypeStruct((SEG * PLAN,), jnp.int32),
        in_specs=[SMEM] * 3,
        out_specs=SMEM,
        cost_estimate=TINY,
        name="plan",
    )(block_pos, block_kind, frame_span)


def pack_kv_kernel(k_ref, v_ref, own_ref, x1_ref, x2_ref, x3_ref, mark_ref):
    _, rank = place()
    mark_ref[...] = k_ref[:16, :D]
    for m, out in enumerate((own_ref, x1_ref, x2_ref, x3_ref)):
        for g in range(2):
            cols = pl.ds(pl.multiple_of((rank ^ m) * (2 * D) + g * D, D), D)
            out[:, 2 * g * D : (2 * g + 1) * D] = k_ref[:, cols]
            out[:, (2 * g + 1) * D : (2 * g + 2) * D] = v_ref[:, cols]


def pack_kv(keys, values):
    return pl.pallas_call(
        pack_kv_kernel,
        out_shape=[bf16(BLK, 4 * D)] * 4 + [bf16(16, D)],
        in_specs=[VMEM, VMEM],
        out_specs=[VMEM] * 5,
        cost_estimate=TINY,
        name="pack_kv",
    )(keys, values)


def pack_q_kernel(q_ref, dep_ref, own_ref, x1_ref, a_ref, b_ref, c_ref, d_ref):
    _, rank = place()
    for out, m, part in ((a_ref, 2, 0), (b_ref, 3, 0), (x1_ref, 1, 0), (own_ref, 0, 0), (c_ref, 2, 1), (d_ref, 3, 1)):
        first = (rank ^ m) * (2 * UNIT) + part * UNIT
        out[...] = q_ref[:, pl.ds(pl.multiple_of(first, UNIT), out.shape[1])]


def pack_q(queries, dep):
    return pl.pallas_call(
        pack_q_kernel,
        out_shape=[bf16(BLK, 2 * UNIT)] * 2 + [bf16(BLK, UNIT)] * 4,
        in_specs=[VMEM, SMEM],
        out_specs=[VMEM] * 6,
        cost_estimate=TINY,
        name="pack_q",
    )(queries, dep)


def gate(value, *deps):
    return pl.pallas_call(
        lambda *refs: None,
        out_shape=jax.ShapeDtypeStruct(value.shape, value.dtype),
        in_specs=[ANY] * (1 + len(deps)),
        out_specs=ANY,
        input_output_aliases={0: 0},
        cost_estimate=TINY,
        name="gate",
    )(value, *deps)


ROWS = HEADS_PER_KV * BLK
TILE = 256
CH = 4
SAFE = 2.0 ** 80


def block_bias(bias, at, count):
    return bias[jnp.where(at >= count, 2, jnp.where(at == 0, 0, 1))]


def weigh_step(width, first, count, q_ref, kv, total, acc, bias):
    keys = kv[pl.ds(first, width), :, :D].reshape(width * BLK, D)
    values = kv[pl.ds(first, width), :, D:].reshape(width * BLK, D)
    more = first > 0

    def score(t):
        return lax.dot_general(q_ref[t : t + TILE], keys, (((1,), (1,)), ((), ())), preferred_element_type=jnp.float32)

    def weigh(t, scores):
        rounded = []
        for r in range(0, TILE, BLK):
            weights = [
                jnp.exp2(scores[r : r + BLK, e * BLK : (e + 1) * BLK] * EXP2_SCALE + block_bias(bias, first + e, count))
                for e in range(width)
            ]
            part = weights[0]
            for w in weights[1:]:
                part = part + w
            rows = slice(t + r, t + r + BLK)
            total[rows] = jnp.where(more, total[rows], 0.0) + part
            rounded.append(jnp.concatenate([w.astype(jnp.bfloat16) for w in weights], axis=1))
        return jnp.concatenate(rounded, axis=0)

    tiles = list(range(0, ROWS, TILE))
    ahead = score(tiles[0])
    for n, t in enumerate(tiles):
        now = ahead
        if n + 1 < len(tiles):
            ahead = score(tiles[n + 1])
        mixed = lax.dot_general(weigh(t, now), values, (((1,), (0,)), ((), ())), preferred_element_type=jnp.float32)
        acc[t : t + TILE] = jnp.where(more, acc[t : t + TILE], 0.0) + mixed


def fast_unit(count, q_ref, kv, total, acc, bias, low, high, o_ref):
    wide = count // CH
    rest = count - wide * CH
    wide = wide + (rest > 2).astype(jnp.int32)

    def step(j, carry):
        weigh_step(CH, CH * j, count, q_ref, kv, total, acc, bias)
        return carry

    lax.fori_loop(0, wide, step, 0)

    @pl.when((rest == 1) | (rest == 2))
    def _():
        weigh_step(2, CH * wide, count, q_ref, kv, total, acc, bias)

    least, most = low[...], high[...]
    for h in range(HEADS_PER_KV):
        r = slice(h * BLK, (h + 1) * BLK)
        weight_sum = jnp.sum(total[r], axis=1, keepdims=True)
        least = jnp.minimum(least, weight_sum)
        most = jnp.maximum(most, weight_sum)
        o_ref[:, h * D : (h + 1) * D] = (acc[r] / weight_sum).astype(jnp.bfloat16)
    low[...] = least
    high[...] = most


def safe_unit(count, q_ref, kv, bias, o_ref):
    chunks = (count + CH - 1) // CH

    def head(h, carry):
        q = q_ref[pl.ds(pl.multiple_of(h * BLK, BLK), BLK)]

        def scaled(j):
            keys = kv[pl.ds(CH * j, CH), :, :D].reshape(CH * BLK, D)
            scores = lax.dot_general(q, keys, (((1,), (1,)), ((), ())), preferred_element_type=jnp.float32)
            return [
                scores[:, e * BLK : (e + 1) * BLK] * EXP2_SCALE + block_bias(bias, CH * j + e, count) for e in range(CH)
            ]

        def largest(j, top):
            for block in scaled(j):
                top = jnp.maximum(top, block)
            return top

        top = lax.fori_loop(0, chunks, largest, jnp.full((BLK, BLK), 2 * NEG, jnp.float32))
        top = jnp.max(top, axis=1, keepdims=True)

        def step(j, carry):
            part, mix = carry
            values = kv[pl.ds(CH * j, CH), :, D:].reshape(CH * BLK, D)
            weights = [jnp.exp2(block - top) for block in scaled(j)]
            for w in weights:
                part = part + w
            rounded = jnp.concatenate([w.astype(jnp.bfloat16) for w in weights], axis=1)
            mix = mix + lax.dot_general(rounded, values, (((1,), (0,)), ((), ())), preferred_element_type=jnp.float32)
            return part, mix

        zero = jnp.zeros((BLK, BLK), jnp.float32)
        part, mix = lax.fori_loop(0, chunks, step, (zero, zero))
        o_ref[:, pl.ds(pl.multiple_of(h * D, D), D)] = (mix / jnp.sum(part, axis=1, keepdims=True)).astype(jnp.bfloat16)
        return carry

    lax.fori_loop(0, HEADS_PER_KV, head, 0)


def attend_kernel(g, units, n_q, has_prev, plan, *refs):
    qs, slots = refs[:n_q], refs[n_q : n_q + SEG]
    out, q_now, kv, total, acc, bias, low, high, o_buf, sems = refs[n_q + SEG + has_prev :]
    _, rank = place()

    def target(i):
        rows = pl.ds(pl.multiple_of((rank ^ units[i][2]) * BLK, BLK), BLK)
        return pltpu.make_async_copy(o_buf.at[i], out.at[rows, g * UNIT : (g + 1) * UNIT], sems.at[i])

    rows = lax.broadcasted_iota(jnp.int32, (BLK, BLK), 0)
    cols = lax.broadcasted_iota(jnp.int32, (BLK, BLK), 1)
    bias[1] = jnp.zeros((BLK, BLK), jnp.float32)
    bias[2] = jnp.full((BLK, BLK), NEG, jnp.float32)
    low[...] = jnp.full((BLK, 1), SAFE, jnp.float32)
    high[...] = jnp.zeros((BLK, 1), jnp.float32)

    def gather(i):
        count, diag = jnp.int32(0), jnp.int32(0)
        for n, (q, part, m) in enumerate(units):
            base = m * PLAN
            count = jnp.where(i == n, plan[base], count)
            diag = jnp.where(i == n, plan[base + 1], diag)

            @pl.when(i == n)
            def _(q=q, part=part, m=m, base=base):
                for h in range(HEADS_PER_KV):
                    q_now[h * BLK : (h + 1) * BLK] = qs[q][:, part * UNIT + h * D : part * UNIT + (h + 1) * D]
                for code in range(WIN):
                    to = plan[base + 2 + code]

                    @pl.when(to >= 0)
                    def _(code=code, to=to):
                        kv[to] = slots[code // SEG][code % SEG]

                rest = lax.rem(plan[base], CH)
                for more in range(CH - 1):
                    @pl.when((rest != 0) & (rest + more < CH))
                    def _(more=more):
                        kv[plan[base] + more] = slots[0][m]

        bias[0] = jnp.where((cols > rows) & (diag > 0), NEG, 0.0)
        return count

    def fast(i, carry):
        count = gather(i)
        fast_unit(count, q_now, kv, total, acc, bias, low, high, o_buf.at[i])
        return carry

    def safe(i, carry):
        count = gather(i)
        safe_unit(count, q_now, kv, bias, o_buf.at[i])
        return carry

    lax.fori_loop(0, len(units), fast, 0)
    inside = (jnp.min(low[...]) > 1 / SAFE) & (jnp.max(high[...]) < SAFE)

    @pl.when(jnp.logical_not(inside))
    def _():
        lax.fori_loop(0, len(units), safe, 0)

    for n in range(len(units)):
        target(n).start()
    for n in range(len(units)):
        target(n).wait()


def attend(plan, g, qs, units, slots, prev):
    operands = [plan, *qs, *slots]
    in_specs = [SMEM] + [VMEM] * (len(qs) + len(slots))
    aliases = {}
    if prev is not None:
        aliases = {len(operands): 0}
        operands.append(prev)
        in_specs.append(ANY)
    n = len(units)
    return pl.pallas_call(
        partial(attend_kernel, g, units, len(qs), int(prev is not None)),
        out_shape=bf16(SEG * BLK, 2 * UNIT),
        in_specs=in_specs,
        out_specs=ANY,
        scratch_shapes=[
            pltpu.VMEM((ROWS, D), jnp.bfloat16),
            pltpu.VMEM((WIN, BLK, 2 * D), jnp.bfloat16),
            pltpu.VMEM((ROWS, BLK), jnp.float32),
            pltpu.VMEM((ROWS, D), jnp.float32),
            pltpu.VMEM((3, BLK, BLK), jnp.float32),
            pltpu.VMEM((BLK, 1), jnp.float32),
            pltpu.VMEM((BLK, 1), jnp.float32),
            pltpu.VMEM((n, BLK, UNIT), jnp.bfloat16),
            pltpu.SemaphoreType.DMA((n,)),
        ],
        input_output_aliases=aliases,
        compiler_params=pltpu.CompilerParams(vmem_limit_bytes=VMEM_LIMIT),
        cost_estimate=TINY,
        name="attend",
    )(*operands)


def body(queries, keys, values, block_pos, block_kind, frame_span):
    groups = lax.axis_size("ctx")
    ranks = lax.axis_size("head")
    y = lax.axis_index("ctx") % 4

    def swap(value, m):
        return lax.ppermute(value, "head", [(i, i ^ m) for i in range(ranks)])

    def ring(value, by):
        return lax.ppermute(value, "ctx", [(i, i // 4 * 4 + (i + by) % 4) for i in range(groups)])

    def plane(value):
        return lax.ppermute(value, "ctx", [(i, (i + 4) % groups) for i in range(groups) if i % 4])

    own, x1, x2, x3, mark = pack_kv(keys, values)
    plan = make_plan(block_pos, block_kind, frame_span)
    q0, q1, a, b, c, d = pack_q(queries, plan)
    from1, from2, from3 = swap(x1, 1), swap(x2, 2), swap(x3, 3)
    pieces = (own, from1, from2, gate(from3, q0))

    def group(g):
        return jnp.stack([piece[:, 2 * g * D : 2 * (g + 1) * D] for piece in pieces])

    def choose(kv, late):
        return jnp.where(y == 3, late, kv), jnp.where(y >= 2, late, kv), jnp.where(y == 0, kv, late)

    def rings(sent):
        return [ring(value, by) for by, value in zip((1, 2, 3), sent)]

    kv0, kv1 = group(0), group(1)
    late0, late1 = plane(kv0), plane(kv1)
    a = swap(gate(a, late0), 2)
    b = swap(gate(b, late1), 3)
    slots0 = [kv0, *rings(choose(kv0, late0))]
    q1 = swap(q1, 1)
    mark = swap(gate(mark, a), 1)
    sent1 = choose(kv1, gate(late1, mark, *slots0[1:]))
    slots1 = [kv1, *rings(sent1)]
    c = swap(gate(c, a), 2)
    d = swap(gate(d, sent1[0]), 3)

    out = attend(plan, 0, (q0, q1), ((0, 0, 0), (1, 0, 1)), slots0, None)
    out = attend(plan, 1, (q0, q1), ((0, 1, 0), (1, 1, 1)), slots1, gate(out, b))
    out = attend(plan, 0, (a, b), ((0, 0, 2), (1, 0, 3)), slots0, out)
    out = attend(plan, 1, (c, d), ((0, 0, 2), (1, 0, 3)), slots1, out)
    return out


def solution(mesh):
    in_specs = (
        P(("ctx", "head"), None),
        P(("ctx", "head"), None),
        P(("ctx", "head"), None),
        P(),
        P("ctx", None),
        P("ctx", None),
    )
    out_specs = P("ctx", "head")
    return jax.shard_map(body, mesh=mesh, in_specs=in_specs, out_specs=out_specs, check_vma=False)
```
